32 devices in a mesh: groups: 2 (over x), tgt: 16 (over z, y, core).
Axes of the slice: x: 2, y: 2, z: 4, core: 2. Of those that a mesh axis runs over, the one named last changes fastest.
Arguments:
- target_features: bfloat16 [32768, 1024], P(('groups', 'tgt')), parts along dimension 0, may hold values from -16 to 16
- source_features: bfloat16 [2048, 1024], P(('groups', 'tgt')), parts along dimension 0, may hold values from -16 to 16
- vectors: bfloat16 [2048, 128], P(('groups', 'tgt')), parts along dimension 0, may hold values from -6 to 6
- current: float32 [32768, 128], P(('groups', 'tgt')), parts along dimension 0, may hold values from -6 to 6
- previous: float32 [32768, 128], P(('groups', 'tgt')), parts along dimension 0, may hold values from -100 to 100
Outputs:
- filtered: float32 [32768, 128], P(('groups', 'tgt')), parts along dimension 0
The draws below stay inside these ranges and needn't reach their ends.
There are 2 independent parts, one for each index of `groups`. The reference program is written for one: setup_inputs(seed, part) draws one part's arguments, and reference() takes and returns one part's arrays. A program takes and returns all parts, laid end to end along the dimension named above; each array names one. Nothing has to cross between parts.
All inputs are finite; a program needn't handle non-finite values.
Results may differ from the reference program's by a relative error of at most 0.002.
Values may be sent and summed in bfloat16 or wider, within the bound.
No kernel may reach another device: no remote copies, remote signals or barrier semaphores. Data moves between devices by JAX's collectives and lax.ppermute only.
A program may use at most 128 MiB of HBM per device.

```python
import math
import jax
import jax.numpy as jnp
from jax import lax

D = 1024
COLS = 128
TGT_DEV = 1024
TARGETS = 16384
SOURCES = 1024


def features_pair(key):
    source = jnp.clip(jax.random.normal(jax.random.fold_in(key, 11), (SOURCES, D), jnp.float32), -6.0, 6.0)
    target = jnp.clip(jax.random.normal(jax.random.fold_in(key, 12), (TARGETS, D), jnp.float32), -6.0, 6.0)
    return (target, source)


def draw_target_features(key, part):
    return features_pair(key)[0].astype(jnp.bfloat16)


def draw_source_features(key, part):
    return features_pair(key)[1].astype(jnp.bfloat16)


def draw_previous(key, part):
    base = jnp.clip(jax.random.normal(jax.random.fold_in(key, 20), (TARGETS, COLS), jnp.float32), -6.0, 6.0)
    ramp = jnp.arange(TARGETS, dtype=jnp.float32) / max(TARGETS - 1, 1)
    row_scale = 0.1 * (1.0 + 2.0 * ramp) * jnp.exp(math.log(10.0) * jax.random.uniform(jax.random.fold_in(key, 21), (TARGETS,), jnp.float32))
    col_scale = 0.3 * jnp.exp(math.log(10.0) * jax.random.uniform(jax.random.fold_in(key, 22), (COLS,), jnp.float32))
    return base * row_scale[:, None] * col_scale[None, :]


def steps_of(key, dims, split, least, largest):
    level, own = 1.0, jax.random.fold_in(key, 6)
    for axis_at, blocks in split:
        draws = jnp.exp(jax.random.uniform(jax.random.fold_in(own, axis_at), (blocks,), jnp.float32, least / len(split), largest / len(split)))
        level = level * jnp.repeat(draws, dims[axis_at] // blocks).reshape([-1 if axis == axis_at else 1 for axis in range(len(dims))])
    return level


def normal_values(rng, extent, width, bound, cuts=(), held_as=jnp.bfloat16):
    drawn = jax.random.normal(rng, extent, jnp.float32) * width
    if len(cuts) > 0:
        drawn = steps_of(rng, extent, cuts, -0.22, 0.18) * drawn
    return jnp.clip(drawn, min=-bound, max=bound).astype(held_as)


def setup_inputs(seed: int = 0, part: int = 0) -> dict:
    key_of = jax.random.split(jax.random.key(seed), 6)
    own_keys = jax.random.split(jax.random.fold_in(key_of[5], part), 6)
    return {
        "target_features": draw_target_features(jax.random.fold_in(jax.random.fold_in(key_of[5], part), 71), part),
        "source_features": draw_source_features(jax.random.fold_in(jax.random.fold_in(key_of[5], part), 71), part),
        "vectors": normal_values(own_keys[2], (SOURCES, COLS), 1.0, 6.0, ((0, 16),)),
        "current": normal_values(own_keys[3], (TARGETS, COLS), 1.0, 6.0, ((0, 16),), jnp.float32),
        "previous": draw_previous(jax.random.fold_in(jax.random.fold_in(key_of[5], part), 71), part),
    }


def block_apply(target_rows, source_features, source_sq, vectors, gamma):
    dots = jnp.dot(target_rows, source_features.T, preferred_element_type=jnp.float32)
    scores = 2.0 * gamma * dots - gamma * source_sq[None, :]
    row_max = lax.optimization_barrier(jnp.max(scores, axis=1, keepdims=True))
    weights = jnp.exp(scores - row_max)
    denominator = lax.optimization_barrier(jnp.sum(weights, axis=1, keepdims=True))
    weights_bf = weights.astype(jnp.bfloat16)
    numer = jnp.dot(weights_bf, vectors, preferred_element_type=jnp.float32)
    return numer / denominator

def reference(target_features, source_features, vectors, current, previous):
    gamma = 0.25 / math.sqrt(D)
    source_float = source_features.astype(jnp.float32)
    source_sq = lax.optimization_barrier(jnp.sum(source_float * source_float, axis=1))
    blocks = target_features.reshape(TARGETS // TGT_DEV, TGT_DEV, D)
    applied = lax.map(lambda rows: block_apply(rows, source_features, source_sq, vectors, gamma), blocks)
    applied = applied.reshape(TARGETS, COLS)
    next_iter = 2.0 / 0.05 * (applied - 0.01 * current) - previous
    column_sq = lax.optimization_barrier(jnp.sum(next_iter * next_iter, axis=0))
    return next_iter / jnp.sqrt(column_sq / TARGETS + 1e-06)
```

```python
import math

import jax
import jax.numpy as jnp
from jax import lax
from jax.sharding import PartitionSpec as P


def swap(x, bits):
    n = lax.axis_size("tgt")
    return lax.ppermute(x, "tgt", [(i, i ^ bits) for i in range(n)])


def gather(shard):
    n = lax.axis_size("tgt")
    if n & (n - 1) or n < 8:
        return lax.all_gather(shard, "tgt", axis=0, tiled=True)
    held = shard
    parts = []
    bit = n // 2
    far = []
    while bit > 4:
        far.append(bit)
        bit //= 2
    for bit in far[:-1]:
        held = jnp.concatenate([held, swap(held, bit)], axis=0)
    parts = [held]
    if far:
        parts.append(swap(held, far[-1]))
    parts = parts + [swap(x, k) for x in parts for k in (4, 2, 6)]
    parts = parts + [swap(x, 1) for x in parts]
    return jnp.concatenate(parts, axis=0)


def total(x):
    n = lax.axis_size("tgt")
    if n & (n - 1):
        return lax.psum(x, "tgt")
    bit = 1
    while bit < n:
        x = x + swap(x, bit)
        bit *= 2
    return x


def block_scores(target_features, feats, gamma):
    feat_float = feats.astype(jnp.float32)
    source_sq = jnp.sum(feat_float * feat_float, axis=1)
    dots = jnp.einsum("td,sd->ts", target_features, feats, preferred_element_type=jnp.float32)
    return 2.0 * gamma * dots - gamma * source_sq[None, :]


def on_device(target_features, source_features, vectors, current, previous):
    width = target_features.shape[1]
    gamma = 0.25 / math.sqrt(width)
    rows = target_features.shape[0]
    everything = gather(jnp.concatenate([source_features, vectors], axis=1))
    all_feats, all_vecs = everything[:, :width], everything[:, width:]
    scores = block_scores(target_features, all_feats, gamma)
    row_max = jnp.max(scores, axis=1, keepdims=True)
    weights = jnp.exp(scores - row_max)
    denominator = jnp.sum(weights, axis=1, keepdims=True)
    numer = jnp.dot(weights.astype(jnp.bfloat16), all_vecs, preferred_element_type=jnp.float32)
    applied = numer / denominator
    next_iter = 2.0 / 0.05 * (applied - 0.01 * current) - previous
    column_sq = total(jnp.sum(next_iter * next_iter, axis=0, keepdims=True))
    total_rows = rows * lax.axis_size("tgt")
    return next_iter / jnp.sqrt(column_sq / total_rows + 1e-06)


def solution(mesh):
    return jax.shard_map(
        on_device,
        mesh=mesh,
        in_specs=(P(("groups", "tgt"), None),) * 5,
        out_specs=P(("groups", "tgt"), None),
        check_vma=False,
    )
```

```python
import functools
import math

import jax
import jax.numpy as jnp
from jax import lax
from jax.experimental import pallas as pl
from jax.experimental.pallas import tpu as pltpu
from jax.sharding import PartitionSpec as P

VMEM = pl.BlockSpec(memory_space=pltpu.VMEM)
ANYWHERE = pl.BlockSpec(memory_space=pl.ANY)


def swap(x, bits):
    n = lax.axis_size("tgt")
    return lax.ppermute(x, "tgt", [(i, i ^ bits) for i in range(n)])


def total(x):
    n = lax.axis_size("tgt")
    if n & (n - 1):
        return lax.psum(x, "tgt")
    bit = 1
    while bit < n:
        x = x + swap(x, bit)
        bit *= 2
    return x


def pack_kernel(feats_ref, vecs_ref, out_ref, sems):
    width = feats_ref.shape[1]
    first = pltpu.make_async_copy(feats_ref, out_ref.at[:, :width], sems.at[0])
    second = pltpu.make_async_copy(vecs_ref, out_ref.at[:, width:], sems.at[1])
    first.start()
    second.start()
    first.wait()
    second.wait()


def pack(feats, vecs):
    rows, width = feats.shape
    return pl.pallas_call(
        pack_kernel,
        out_shape=jax.ShapeDtypeStruct((rows, width + vecs.shape[1]), feats.dtype),
        in_specs=[ANYWHERE] * 2,
        out_specs=VMEM,
        scratch_shapes=[pltpu.SemaphoreType.DMA((2,))],
        compiler_params=pltpu.CompilerParams(vmem_limit_bytes=4 * 2**20),
    )(feats, vecs)


def block(target, packed, scale):
    width = target.shape[1]
    feats = packed[:, :width]
    return lax.dot_general(target, feats, (((1,), (1,)), ((), ())), preferred_element_type=jnp.float32) * scale


def square_sums(packed, width, scale):
    feats = packed[:, :width].astype(jnp.float32)
    square = feats * feats
    high = square.astype(jnp.bfloat16)
    low = (square - high.astype(jnp.float32)).astype(jnp.bfloat16)
    ones = jnp.ones((8, width), jnp.bfloat16)
    over = functools.partial(
        lax.dot_general, dimension_numbers=(((1,), (1,)), ((), ())), preferred_element_type=jnp.float32
    )
    return (over(ones, high) + over(ones, low))[:1] * (0.5 * scale)


def first_kernel(tile, scale, count, target_ref, *refs):
    packed_refs, (top_ref, denom_ref, numer_ref) = refs[:count], refs[count:]
    width = target_ref.shape[1]
    packed = jnp.concatenate([r[...] for r in packed_refs], axis=0)
    offset = square_sums(packed, width, scale)
    vecs = packed[:, width:]
    for at in range(0, target_ref.shape[0], tile):
        rows = pl.ds(at, tile)
        scores = block(target_ref[rows, :], packed, scale) - offset
        top = jnp.max(scores, axis=1, keepdims=True)
        weights = jnp.exp2(scores - top)
        top_ref[rows, :] = jnp.broadcast_to(top, (tile, top_ref.shape[1]))
        denom_ref[rows, :] = jnp.broadcast_to(jnp.sum(weights, axis=1, keepdims=True), (tile, denom_ref.shape[1]))
        numer_ref[rows, :] = jnp.dot(weights.astype(jnp.bfloat16), vecs, preferred_element_type=jnp.float32)


def last_kernel(tile, scale, count, target_ref, top_ref, denom_ref, numer_ref, current_ref, previous_ref, *refs):
    packed_refs, (next_ref, column_ref) = refs[:count], refs[count:]
    width = target_ref.shape[1]
    packed = jnp.concatenate([r[...] for r in packed_refs], axis=0)
    offset = square_sums(packed, width, scale)
    vecs = packed[:, width:]
    column = jnp.zeros((8, vecs.shape[1]), jnp.float32)
    for at in range(0, target_ref.shape[0], tile):
        rows = pl.ds(at, tile)
        scores = block(target_ref[rows, :], packed, scale) - offset
        before = top_ref[rows, :1]
        top = jnp.maximum(before, jnp.max(scores, axis=1, keepdims=True))
        weights = jnp.exp2(scores - top)
        shrink = jnp.exp2(before - top)
        denom = shrink * denom_ref[rows, :1] + jnp.sum(weights, axis=1, keepdims=True)
        numer = shrink * numer_ref[rows, :] + jnp.dot(
            weights.astype(jnp.bfloat16), vecs, preferred_element_type=jnp.float32
        )
        step = 2.0 / 0.05 * (numer / denom - 0.01 * current_ref[rows, :]) - previous_ref[rows, :]
        next_ref[rows, :] = step
        column = column + jnp.sum((step * step).reshape(tile // 8, 8, -1), axis=0)
    column_ref[...] = jnp.sum(column, axis=0, keepdims=True)


def cost(rows, width, cols, sources):
    return pl.CostEstimate(
        flops=2 * rows * sources * (width + cols), bytes_accessed=2 * rows * width, transcendentals=rows * sources
    )


def first_part(target, pieces, scale):
    rows, width = target.shape
    cols = pieces[0].shape[1] - width
    sources = sum(p.shape[0] for p in pieces)
    return pl.pallas_call(
        functools.partial(first_kernel, min(rows, 256), scale, len(pieces)),
        out_shape=[jax.ShapeDtypeStruct((rows, cols), jnp.float32)] * 3,
        in_specs=[VMEM] * (1 + len(pieces)),
        out_specs=[VMEM] * 3,
        compiler_params=pltpu.CompilerParams(vmem_limit_bytes=20 * 2**20),
        cost_estimate=cost(rows, width, cols, sources),
    )(target, *pieces)


def last_part(target, state, current, previous, pieces, scale):
    rows, width = target.shape
    cols = current.shape[1]
    sources = sum(p.shape[0] for p in pieces)
    return pl.pallas_call(
        functools.partial(last_kernel, min(rows, 256), scale, len(pieces)),
        out_shape=[jax.ShapeDtypeStruct((rows, cols), jnp.float32), jax.ShapeDtypeStruct((1, cols), jnp.float32)],
        in_specs=[VMEM] * (6 + len(pieces)),
        out_specs=[VMEM] * 2,
        compiler_params=pltpu.CompilerParams(vmem_limit_bytes=20 * 2**20),
        cost_estimate=cost(rows, width, cols, sources),
    )(target, *state, current, previous, *pieces)


def gather(shard):
    n = lax.axis_size("tgt")
    if n & (n - 1) or n < 16:
        everything = lax.all_gather(shard, "tgt", axis=0, tiled=True)
        half = everything.shape[0] // 2
        return [everything[:half]], [everything[half:]]
    near, bit = shard, n // 2
    while bit > 8:
        near = jnp.concatenate([near, swap(near, bit)], axis=0)
        bit //= 2
    far = swap(near, bit)
    around = [swap(near, k) for k in (4, 2, 6)]
    beyond = [swap(far, k) for k in (4, 2, 6)]
    early = [near] + around + [far]
    early = early + [swap(x, 1) for x in early]
    late = beyond + [swap(x, 1) for x in beyond]
    return early, late


def on_device(target_features, source_features, vectors, current, previous):
    rows, width = target_features.shape
    gamma = 0.25 / math.sqrt(width)
    scale = 2.0 * gamma * math.log2(math.e)
    early, late = gather(pack(source_features, vectors))
    state = first_part(target_features, early, scale)
    next_iter, column = last_part(target_features, state, current, previous, late, scale)
    column_sq = total(column)
    total_rows = rows * lax.axis_size("tgt")
    return next_iter / jnp.sqrt(column_sq / total_rows + 1e-06)


def solution(mesh):
    return jax.shard_map(
        on_device,
        mesh=mesh,
        in_specs=(P(("groups", "tgt"), None),) * 5,
        out_specs=P(("groups", "tgt"), None),
        check_vma=False,
    )
```

```python
import functools
import math

import jax
import jax.numpy as jnp
from jax import lax
from jax.experimental import pallas as pl
from jax.experimental.pallas import tpu as pltpu
from jax.sharding import PartitionSpec as P

VMEM = pl.BlockSpec(memory_space=pltpu.VMEM)
SMALL = pl.CostEstimate(flops=1, bytes_accessed=1, transcendentals=0)
IN_HBM = pl.BlockSpec(memory_space=pltpu.HBM)


def hbm(x):
    return pltpu.with_memory_space_constraint(x, pltpu.HBM)


def swap(x, bits):
    n = lax.axis_size("tgt")
    return lax.ppermute(x, "tgt", [(i, i ^ bits) for i in range(n)])


def total(x):
    n = lax.axis_size("tgt")
    if n & (n - 1):
        return lax.psum(x, "tgt")
    bit = 1
    while bit < n:
        x = x + swap(x, bit)
        bit *= 2
    return x


def pack_kernel(feats_ref, vecs_ref, out_ref, sems):
    width = feats_ref.shape[1]
    first = pltpu.make_async_copy(feats_ref, out_ref.at[:, :width], sems.at[0])
    second = pltpu.make_async_copy(vecs_ref, out_ref.at[:, width:], sems.at[1])
    first.start()
    second.start()
    first.wait()
    second.wait()


def pack(feats, vecs):
    rows, width = feats.shape
    return pl.pallas_call(
        pack_kernel,
        out_shape=jax.ShapeDtypeStruct((rows, width + vecs.shape[1]), feats.dtype),
        in_specs=[IN_HBM] * 2,
        out_specs=VMEM,
        scratch_shapes=[pltpu.SemaphoreType.DMA((2,))],
        compiler_params=pltpu.CompilerParams(vmem_limit_bytes=4 * 2**20),
    )(hbm(feats), hbm(vecs))


def join_kernel(count, *refs):
    out_ref = refs[-1]
    at = 0
    for piece in refs[:count]:
        out_ref[at : at + piece.shape[0], :] = piece[...]
        at += piece.shape[0]


def joined(pieces, *tokens):
    rows = sum(p.shape[0] for p in pieces)
    return pl.pallas_call(
        functools.partial(join_kernel, len(pieces)),
        out_shape=jax.ShapeDtypeStruct((rows, pieces[0].shape[1]), pieces[0].dtype),
        in_specs=[VMEM] * len(pieces) + [pl.BlockSpec(memory_space=pl.ANY)] * len(tokens),
        out_specs=VMEM,
        compiler_params=pltpu.CompilerParams(vmem_limit_bytes=8 * 2**20),
        cost_estimate=SMALL,
    )(*pieces, *tokens)


def tie(x, *tokens):
    return joined([x], *tokens)


def load_kernel(array_ref, token_ref, out_ref, sem):
    del token_ref
    parts = sem.shape[0]
    rows = array_ref.shape[0] // parts
    copies = [
        pltpu.make_async_copy(array_ref.at[pl.ds(k * rows, rows)], out_ref.at[pl.ds(k * rows, rows)], sem.at[k])
        for k in range(parts)
    ]
    for copy in copies:
        copy.start()
    for copy in copies:
        copy.wait()


def load(array, token):
    return pl.pallas_call(
        load_kernel,
        out_shape=jax.ShapeDtypeStruct(array.shape, array.dtype),
        in_specs=[IN_HBM, pl.BlockSpec(memory_space=pl.ANY)],
        out_specs=VMEM,
        scratch_shapes=[pltpu.SemaphoreType.DMA((8 if array.shape[0] % 128 == 0 else 1,))],
        compiler_params=pltpu.CompilerParams(vmem_limit_bytes=4 * 2**20),
        cost_estimate=SMALL,
    )(hbm(array), token)


def scores_of(target, feats):
    wide = feats.astype(jnp.float32)
    square = wide * wide
    lanes = min(128, square.shape[1])
    part = square[:, :lanes]
    for at in range(lanes, square.shape[1], lanes):
        part = part + square[:, at : at + lanes]
    half = 0.5 * jnp.sum(part.T, axis=0, keepdims=True)
    dots = lax.dot_general(target, feats, (((1,), (1,)), ((), ())), preferred_element_type=jnp.float32)
    return dots - half


def step_kernel(scale, count, first, last, target_ref, *refs):
    pieces, refs = refs[:count], refs[count:]
    width = target_ref.shape[1]
    packed = jnp.concatenate([r[...] for r in pieces], axis=0)
    vecs = packed[:, width:]
    scores = scores_of(target_ref[...], packed[:, :width])
    top = jnp.max(scores, axis=1, keepdims=True)
    top = jnp.broadcast_to(top, (scores.shape[0], vecs.shape[1]))
    if not first:
        (before, denom, numer), refs = [r[...] for r in refs[:3]], refs[3:]
        top = jnp.maximum(before, top)
    across = scores.shape[1]
    level = jnp.concatenate([top] * pl.cdiv(across, top.shape[1]), axis=1)[:, :across]
    weights = jnp.exp2((scores - level) * scale)
    added = jnp.broadcast_to(jnp.sum(weights, axis=1, keepdims=True), top.shape)
    product = jnp.dot(weights.astype(jnp.bfloat16), vecs, preferred_element_type=jnp.float32)
    if not first:
        shrink = jnp.exp2((before - top) * scale)
        added = shrink * denom + added
        product = shrink * numer + product
    if not last:
        top_ref, denom_ref, numer_ref = refs
        top_ref[...] = top
        denom_ref[...] = added
        numer_ref[...] = product
        return
    current_ref, previous_ref, next_ref, column_ref = refs
    step = 2.0 / 0.05 * (product / added - 0.01 * current_ref[...]) - previous_ref[...]
    next_ref[...] = step
    column_ref[...] = jnp.sum(step * step, axis=0, keepdims=True)


def step(target, pieces, state, ends, scale):
    rows, width = target.shape
    cols = pieces[0].shape[1] - width
    whole = jax.ShapeDtypeStruct((rows, cols), jnp.float32)
    return pl.pallas_call(
        functools.partial(step_kernel, scale, len(pieces), not state, bool(ends)),
        out_shape=[whole, jax.ShapeDtypeStruct((1, cols), jnp.float32)] if ends else [whole] * 3,
        in_specs=[VMEM] * (1 + len(pieces) + len(state) + len(ends)),
        out_specs=[VMEM] * (2 if ends else 3),
        compiler_params=pltpu.CompilerParams(vmem_limit_bytes=20 * 2**20),
        cost_estimate=SMALL,
    )(target, *pieces, *state, *ends)


def gather(shard, target, scale):
    n = lax.axis_size("tgt")
    if n & (n - 1) or n < 16:
        everything = lax.all_gather(shard, "tgt", axis=0, tiled=True)
        return target, [everything], []
    near, bit = shard, n // 2
    while bit > 8:
        near = jnp.concatenate([near, swap(near, bit)], axis=0)
        bit //= 2
    near_other = swap(near, 1)
    far = swap(near, bit)
    later = tie(near, near_other)
    around = [swap(later, k) for k in (4, 2, 6)]
    target = load(target, later)
    beyond = [swap(far, k) for k in (4, 2, 6)]
    state = step(target, [near, near_other] + around + [far], [], [], scale)
    own = joined(around + [far], state[0])
    state = step(target, beyond, state, [], scale)
    return target, [swap(own, 1), swap(joined(beyond), 1)], state


def on_device(target_features, source_features, vectors, current, previous):
    rows, width = target_features.shape
    gamma = 0.25 / math.sqrt(width)
    scale = 2.0 * gamma * math.log2(math.e)
    target, pieces, state = gather(pack(source_features, vectors), target_features, scale)
    next_iter, column = step(target, pieces, state, [current, previous], scale)
    column_sq = total(column)
    total_rows = rows * lax.axis_size("tgt")
    return next_iter / jnp.sqrt(column_sq / total_rows + 1e-06)


def solution(mesh):
    return jax.shard_map(
        on_device,
        mesh=mesh,
        in_specs=(P(("groups", "tgt"), None),) * 5,
        out_specs=P(("groups", "tgt"), None),
        check_vma=False,
    )
```

```python
import functools
import math

import jax
import jax.numpy as jnp
from jax import lax
from jax.experimental import pallas as pl
from jax.experimental.pallas import tpu as pltpu
from jax.sharding import PartitionSpec as P

VMEM = pl.BlockSpec(memory_space=pltpu.VMEM)
SMALL = pl.CostEstimate(flops=1, bytes_accessed=1, transcendentals=0)
IN_HBM = pl.BlockSpec(memory_space=pltpu.HBM)


def hbm(x):
    return pltpu.with_memory_space_constraint(x, pltpu.HBM)


def swap(x, bits):
    n = lax.axis_size("tgt")
    return lax.ppermute(x, "tgt", [(i, i ^ bits) for i in range(n)])


def cross(x, low, high, ends_first):
    n = lax.axis_size("tgt")
    pairs = []
    for i in range(n):
        at_end = (i // low + i // high) % 2 == 0
        pairs.append((i, i ^ (low if at_end == ends_first else high)))
    return lax.ppermute(x, "tgt", pairs)


def total(x):
    n = lax.axis_size("tgt")
    if n & (n - 1) or n < 16:
        return lax.psum(x, "tgt")
    x = x + swap(x, 1)
    x = x + sum(swap(x, k) for k in (2, 4, 6))
    bit = 8
    while bit < n:
        x = x + swap(x, bit)
        bit *= 2
    return x


def pack_kernel(feats_ref, vecs_ref, out_ref, sems):
    width = feats_ref.shape[1]
    first = pltpu.make_async_copy(feats_ref, out_ref.at[:, :width], sems.at[0])
    second = pltpu.make_async_copy(vecs_ref, out_ref.at[:, width:], sems.at[1])
    first.start()
    second.start()
    first.wait()
    second.wait()


def pack(feats, vecs):
    rows, width = feats.shape
    return pl.pallas_call(
        pack_kernel,
        out_shape=jax.ShapeDtypeStruct((rows, width + vecs.shape[1]), feats.dtype),
        in_specs=[IN_HBM] * 2,
        out_specs=VMEM,
        scratch_shapes=[pltpu.SemaphoreType.DMA((2,))],
        compiler_params=pltpu.CompilerParams(vmem_limit_bytes=4 * 2**20),
    )(hbm(feats), hbm(vecs))


def join_kernel(count, *refs):
    out_ref = refs[-1]
    at = 0
    for piece in refs[:count]:
        out_ref[at : at + piece.shape[0], :] = piece[...]
        at += piece.shape[0]


def joined(pieces, *tokens):
    rows = sum(p.shape[0] for p in pieces)
    return pl.pallas_call(
        functools.partial(join_kernel, len(pieces)),
        out_shape=jax.ShapeDtypeStruct((rows, pieces[0].shape[1]), pieces[0].dtype),
        in_specs=[VMEM] * len(pieces) + [pl.BlockSpec(memory_space=pl.ANY)] * len(tokens),
        out_specs=VMEM,
        compiler_params=pltpu.CompilerParams(vmem_limit_bytes=8 * 2**20),
        cost_estimate=SMALL,
    )(*pieces, *tokens)


def tie(x, *tokens):
    return joined([x], *tokens)


def load_kernel(array_ref, token_ref, out_ref, sem):
    del token_ref
    parts = sem.shape[0]
    rows = array_ref.shape[0] // parts
    copies = [
        pltpu.make_async_copy(array_ref.at[pl.ds(k * rows, rows)], out_ref.at[pl.ds(k * rows, rows)], sem.at[k])
        for k in range(parts)
    ]
    for copy in copies:
        copy.start()
    for copy in copies:
        copy.wait()


def load(array, token):
    return pl.pallas_call(
        load_kernel,
        out_shape=jax.ShapeDtypeStruct(array.shape, array.dtype),
        in_specs=[IN_HBM, pl.BlockSpec(memory_space=pl.ANY)],
        out_specs=VMEM,
        scratch_shapes=[pltpu.SemaphoreType.DMA((8 if array.shape[0] % 128 == 0 else 1,))],
        compiler_params=pltpu.CompilerParams(vmem_limit_bytes=4 * 2**20),
        cost_estimate=SMALL,
    )(hbm(array), token)


def scores_of(target, feats):
    wide = feats.astype(jnp.float32)
    square = wide * wide
    lanes = min(128, square.shape[1])
    part = square[:, :lanes]
    for at in range(lanes, square.shape[1], lanes):
        part = part + square[:, at : at + lanes]
    half = 0.5 * jnp.sum(part.T, axis=0, keepdims=True)
    dots = lax.dot_general(target, feats, (((1,), (1,)), ((), ())), preferred_element_type=jnp.float32)
    return dots - half


def step_kernel(scale, count, first, last, target_ref, *refs):
    pieces, refs = refs[:count], refs[count:]
    width = target_ref.shape[1]
    packed = jnp.concatenate([r[...] for r in pieces], axis=0)
    vecs = packed[:, width:]
    scores = scores_of(target_ref[...], packed[:, :width])
    top = jnp.max(scores, axis=1, keepdims=True)
    top = jnp.broadcast_to(top, (scores.shape[0], vecs.shape[1]))
    if not first:
        (before, denom, numer), refs = [r[...] for r in refs[:3]], refs[3:]
        top = jnp.maximum(before, top)
    across = scores.shape[1]
    level = jnp.concatenate([top] * pl.cdiv(across, top.shape[1]), axis=1)[:, :across]
    weights = jnp.exp2((scores - level) * scale)
    added = jnp.broadcast_to(jnp.sum(weights, axis=1, keepdims=True), top.shape)
    product = jnp.dot(weights.astype(jnp.bfloat16), vecs, preferred_element_type=jnp.float32)
    if not first:
        shrink = jnp.exp2((before - top) * scale)
        added = shrink * denom + added
        product = shrink * numer + product
    if not last:
        top_ref, denom_ref, numer_ref = refs
        top_ref[...] = top
        denom_ref[...] = added
        numer_ref[...] = product
        return
    current_ref, previous_ref, next_ref, column_ref = refs
    step = 2.0 / 0.05 * (product / added - 0.01 * current_ref[...]) - previous_ref[...]
    next_ref[...] = step
    column_ref[...] = jnp.sum(step * step, axis=0, keepdims=True)


def step(target, pieces, state, ends, scale, micros=0):
    rows, width = target.shape
    cols = pieces[0].shape[1] - width
    whole = jax.ShapeDtypeStruct((rows, cols), jnp.float32)
    return pl.pallas_call(
        functools.partial(step_kernel, scale, len(pieces), not state, bool(ends)),
        out_shape=[whole, jax.ShapeDtypeStruct((1, cols), jnp.float32)] if ends else [whole] * 3,
        in_specs=[VMEM] * (1 + len(pieces) + len(state) + len(ends)),
        out_specs=[VMEM] * (2 if ends else 3),
        compiler_params=pltpu.CompilerParams(vmem_limit_bytes=20 * 2**20),
        cost_estimate=pl.CostEstimate(flops=1 + micros * 10**9, bytes_accessed=1, transcendentals=0),
    )(target, *pieces, *state, *ends)


def gather(shard, target, scale):
    n = lax.axis_size("tgt")
    if n & (n - 1) or n < 16:
        everything = lax.all_gather(shard, "tgt", axis=0, tiled=True)
        return target, [everything], []
    near, bit = shard, n // 2
    while bit > 8:
        near = jnp.concatenate([near, swap(near, bit)], axis=0)
        bit //= 2
    near_other = swap(near, 1)
    one = cross(near, 4, bit, True)
    later = tie(near, near_other)
    two = cross(later, 4, bit, False)
    around = [one, two] + [swap(later, k) for k in (2, 6)]
    target = load(target, later)
    place = lax.axis_index("tgt")
    far = jnp.where((place // 4 + place // bit) % 2 == 0, one, two)
    beyond = [swap(far, k) for k in (4, 2, 6)]
    state = step(target, [near, near_other] + around, [], [], scale, 20)
    early = swap(joined(around), 1)
    state = step(target, [early], state, [], scale, 20)
    own = joined(beyond, state[0])
    state = step(target, [own], state, [], scale, 20)
    return target, [swap(own, 1)], state


def on_device(target_features, source_features, vectors, current, previous):
    rows, width = target_features.shape
    gamma = 0.25 / math.sqrt(width)
    scale = 2.0 * gamma * math.log2(math.e)
    target, pieces, state = gather(pack(source_features, vectors), target_features, scale)
    next_iter, column = step(target, pieces, state, [current, previous], scale)
    column_sq = total(column)
    total_rows = rows * lax.axis_size("tgt")
    return next_iter / jnp.sqrt(column_sq / total_rows + 1e-06)


def solution(mesh):
    return jax.shard_map(
        on_device,
        mesh=mesh,
        in_specs=(P(("groups", "tgt"), None),) * 5,
        out_specs=P(("groups", "tgt"), None),
        check_vma=False,
    )
```

```python
import functools
import math

import jax
import jax.numpy as jnp
from jax import lax
from jax.experimental import pallas as pl
from jax.experimental.pallas import tpu as pltpu
from jax.sharding import PartitionSpec as P

VMEM = pl.BlockSpec(memory_space=pltpu.VMEM)
SMALL = pl.CostEstimate(flops=1, bytes_accessed=1, transcendentals=0)
IN_HBM = pl.BlockSpec(memory_space=pltpu.HBM)


def hbm(x):
    return pltpu.with_memory_space_constraint(x, pltpu.HBM)


def swap(x, bits):
    n = lax.axis_size("tgt")
    return lax.ppermute(x, "tgt", [(i, i ^ bits) for i in range(n)])


def cross(x, low, high, ends_first):
    n = lax.axis_size("tgt")
    pairs = []
    for i in range(n):
        at_end = (i // low + i // high) % 2 == 0
        pairs.append((i, i ^ (low if at_end == ends_first else high)))
    return lax.ppermute(x, "tgt", pairs)


def total(x):
    n = lax.axis_size("tgt")
    if n & (n - 1) or n < 16:
        return lax.psum(x, "tgt")
    x = x + swap(x, 1)
    x = x + sum(swap(x, k) for k in (2, 4, 6))
    bit = 8
    while bit < n:
        x = x + swap(x, bit)
        bit *= 2
    return x


def pack_kernel(feats_ref, vecs_ref, out_ref, sems):
    width = feats_ref.shape[1]
    first = pltpu.make_async_copy(feats_ref, out_ref.at[:, :width], sems.at[0])
    second = pltpu.make_async_copy(vecs_ref, out_ref.at[:, width:], sems.at[1])
    first.start()
    second.start()
    first.wait()
    second.wait()


def pack(feats, vecs):
    rows, width = feats.shape
    return pl.pallas_call(
        pack_kernel,
        out_shape=jax.ShapeDtypeStruct((rows, width + vecs.shape[1]), feats.dtype),
        in_specs=[IN_HBM] * 2,
        out_specs=VMEM,
        scratch_shapes=[pltpu.SemaphoreType.DMA((2,))],
        compiler_params=pltpu.CompilerParams(vmem_limit_bytes=4 * 2**20),
    )(hbm(feats), hbm(vecs))


def join_kernel(count, *refs):
    out_ref = refs[-1]
    at = 0
    for piece in refs[:count]:
        out_ref[at : at + piece.shape[0], :] = piece[...]
        at += piece.shape[0]


def joined(pieces, *tokens):
    rows = sum(p.shape[0] for p in pieces)
    return pl.pallas_call(
        functools.partial(join_kernel, len(pieces)),
        out_shape=jax.ShapeDtypeStruct((rows, pieces[0].shape[1]), pieces[0].dtype),
        in_specs=[VMEM] * len(pieces) + [pl.BlockSpec(memory_space=pl.ANY)] * len(tokens),
        out_specs=VMEM,
        compiler_params=pltpu.CompilerParams(vmem_limit_bytes=8 * 2**20),
        cost_estimate=SMALL,
    )(*pieces, *tokens)


def tie(x, *tokens):
    return joined([x], *tokens)


def load_kernel(array_ref, token_ref, out_ref, sem):
    del token_ref
    parts = sem.shape[0]
    rows = array_ref.shape[0] // parts
    copies = [
        pltpu.make_async_copy(array_ref.at[pl.ds(k * rows, rows)], out_ref.at[pl.ds(k * rows, rows)], sem.at[k])
        for k in range(parts)
    ]
    for copy in copies:
        copy.start()
    for copy in copies:
        copy.wait()


def load(array, token):
    return pl.pallas_call(
        load_kernel,
        out_shape=jax.ShapeDtypeStruct(array.shape, array.dtype),
        in_specs=[IN_HBM, pl.BlockSpec(memory_space=pl.ANY)],
        out_specs=VMEM,
        scratch_shapes=[pltpu.SemaphoreType.DMA((8 if array.shape[0] % 128 == 0 else 1,))],
        compiler_params=pltpu.CompilerParams(vmem_limit_bytes=4 * 2**20),
        cost_estimate=SMALL,
    )(hbm(array), token)


def scores_of(target, feats):
    wide = feats.astype(jnp.float32)
    square = wide * wide
    lanes = min(128, square.shape[1])
    part = square[:, :lanes]
    for at in range(lanes, square.shape[1], lanes):
        part = part + square[:, at : at + lanes]
    half = 0.5 * jnp.sum(part.T, axis=0, keepdims=True)
    dots = lax.dot_general(target, feats, (((1,), (1,)), ((), ())), preferred_element_type=jnp.float32)
    return dots - half


def step_kernel(scale, count, first, last, exact, target_ref, *refs):
    pieces, refs = refs[:count], refs[count:]
    width = target_ref.shape[1]
    packed = jnp.concatenate([r[...] for r in pieces], axis=0)
    vecs = packed[:, width:]
    scores = scores_of(target_ref[...], packed[:, :width])
    top = jnp.max(scores, axis=1, keepdims=True)
    top = jnp.broadcast_to(top, (scores.shape[0], vecs.shape[1]))
    if not first:
        (before, denom, numer), refs = [r[...] for r in refs[:3]], refs[3:]
        top = jnp.maximum(before, top)
    across = scores.shape[1]
    level = jnp.concatenate([top] * pl.cdiv(across, top.shape[1]), axis=1)[:, :across]
    weights = jnp.exp2((scores - level) * scale)
    added = jnp.broadcast_to(jnp.sum(weights, axis=1, keepdims=True), top.shape)
    high = weights.astype(jnp.bfloat16)
    product = jnp.dot(high, vecs, preferred_element_type=jnp.float32)
    if exact:
        low = (weights - high.astype(jnp.float32)).astype(jnp.bfloat16)
        product = product + jnp.dot(low, vecs, preferred_element_type=jnp.float32)
    if not first:
        shrink = jnp.exp2((before - top) * scale)
        added = shrink * denom + added
        product = shrink * numer + product
    if not last:
        top_ref, denom_ref, numer_ref = refs
        top_ref[...] = top
        denom_ref[...] = added
        numer_ref[...] = product
        return
    current_ref, previous_ref, next_ref, column_ref = refs
    step = 2.0 / 0.05 * (product / added - 0.01 * current_ref[...]) - previous_ref[...]
    next_ref[...] = step
    column_ref[...] = jnp.sum(step * step, axis=0, keepdims=True)


def step(target, pieces, state, ends, scale, micros=0, exact=False):
    rows, width = target.shape
    cols = pieces[0].shape[1] - width
    whole = jax.ShapeDtypeStruct((rows, cols), jnp.float32)
    return pl.pallas_call(
        functools.partial(step_kernel, scale, len(pieces), not state, bool(ends), exact),
        out_shape=[whole, jax.ShapeDtypeStruct((1, cols), jnp.float32)] if ends else [whole] * 3,
        in_specs=[VMEM] * (1 + len(pieces) + len(state) + len(ends)),
        out_specs=[VMEM] * (2 if ends else 3),
        compiler_params=pltpu.CompilerParams(vmem_limit_bytes=20 * 2**20),
        cost_estimate=pl.CostEstimate(flops=1 + micros * 10**9, bytes_accessed=1, transcendentals=0),
    )(target, *pieces, *state, *ends)


def gather(shard, target, scale):
    n = lax.axis_size("tgt")
    if n & (n - 1) or n < 16:
        everything = lax.all_gather(shard, "tgt", axis=0, tiled=True)
        return target, [everything], []
    near, bit = shard, n // 2
    while bit > 8:
        near = jnp.concatenate([near, swap(near, bit)], axis=0)
        bit //= 2
    near_other = swap(near, 1)
    one = cross(near, 4, bit, True)
    later = tie(near, near_other)
    two = cross(later, 4, bit, False)
    around = [one, two] + [swap(later, k) for k in (2, 6)]
    target = load(target, later)
    place = lax.axis_index("tgt")
    far = jnp.where((place // 4 + place // bit) % 2 == 0, one, two)
    beyond = [swap(far, k) for k in (4, 2, 6)]
    state = step(target, [near, near_other] + around, [], [], scale, 20, True)
    early = swap(joined(around), 1)
    state = step(target, [early], state, [], scale, 20, True)
    others = [swap(joined(beyond[:2], state[0]), 1), swap(beyond[2], 1)]
    state = step(target, beyond, state, [], scale, 0)
    return target, others, state


def on_device(target_features, source_features, vectors, current, previous):
    rows, width = target_features.shape
    gamma = 0.25 / math.sqrt(width)
    scale = 2.0 * gamma * math.log2(math.e)
    target, pieces, state = gather(pack(source_features, vectors), target_features, scale)
    next_iter, column = step(target, pieces, state, [current, previous], scale)
    column_sq = total(column)
    total_rows = rows * lax.axis_size("tgt")
    return next_iter / jnp.sqrt(column_sq / total_rows + 1e-06)


def solution(mesh):
    return jax.shard_map(
        on_device,
        mesh=mesh,
        in_specs=(P(("groups", "tgt"), None),) * 5,
        out_specs=P(("groups", "tgt"), None),
        check_vma=False,
    )
```

```python
import functools
import math

import jax
import jax.numpy as jnp
from jax import lax
from jax.experimental import pallas as pl
from jax.experimental.pallas import tpu as pltpu
from jax.sharding import PartitionSpec as P

VMEM = pl.BlockSpec(memory_space=pltpu.VMEM)
SMALL = pl.CostEstimate(flops=1, bytes_accessed=1, transcendentals=0)
IN_HBM = pl.BlockSpec(memory_space=pltpu.HBM)


def hbm(x):
    return pltpu.with_memory_space_constraint(x, pltpu.HBM)


def swap(x, bits):
    n = lax.axis_size("tgt")
    return lax.ppermute(x, "tgt", [(i, i ^ bits) for i in range(n)])


def swap_by_core(x, first, second):
    n = lax.axis_size("tgt")
    return lax.ppermute(x, "tgt", [(i, i ^ (second if i % 2 else first)) for i in range(n)])


def cross(x, low, high, ends_first):
    n = lax.axis_size("tgt")
    pairs = []
    for i in range(n):
        at_end = (i // low + i // high) % 2 == 0
        pairs.append((i, i ^ (low if at_end == ends_first else high)))
    return lax.ppermute(x, "tgt", pairs)


def total(x):
    n = lax.axis_size("tgt")
    if n & (n - 1) or n < 16:
        return lax.psum(x, "tgt")
    x = x + swap(x, 1)
    x = x + sum(swap(x, k) for k in (2, 4, 6))
    bit = 8
    while bit < n:
        x = x + swap(x, bit)
        bit *= 2
    return x


def pack_kernel(feats_ref, vecs_ref, out_ref, sems):
    width = feats_ref.shape[1]
    first = pltpu.make_async_copy(feats_ref, out_ref.at[:, :width], sems.at[0])
    second = pltpu.make_async_copy(vecs_ref, out_ref.at[:, width:], sems.at[1])
    first.start()
    second.start()
    first.wait()
    second.wait()


def pack(feats, vecs):
    rows, width = feats.shape
    return pl.pallas_call(
        pack_kernel,
        out_shape=jax.ShapeDtypeStruct((rows, width + vecs.shape[1]), feats.dtype),
        in_specs=[IN_HBM] * 2,
        out_specs=VMEM,
        scratch_shapes=[pltpu.SemaphoreType.DMA((2,))],
        compiler_params=pltpu.CompilerParams(vmem_limit_bytes=4 * 2**20),
    )(hbm(feats), hbm(vecs))


def join_kernel(count, *refs):
    out_ref = refs[-1]
    at = 0
    for piece in refs[:count]:
        out_ref[at : at + piece.shape[0], :] = piece[...]
        at += piece.shape[0]


def joined(pieces, *tokens):
    rows = sum(p.shape[0] for p in pieces)
    return pl.pallas_call(
        functools.partial(join_kernel, len(pieces)),
        out_shape=jax.ShapeDtypeStruct((rows, pieces[0].shape[1]), pieces[0].dtype),
        in_specs=[VMEM] * len(pieces) + [pl.BlockSpec(memory_space=pl.ANY)] * len(tokens),
        out_specs=VMEM,
        compiler_params=pltpu.CompilerParams(vmem_limit_bytes=8 * 2**20),
        cost_estimate=SMALL,
    )(*pieces, *tokens)


def tie(x, *tokens):
    return joined([x], *tokens)


def load_kernel(array_ref, token_ref, out_ref, sem):
    del token_ref
    parts = sem.shape[0]
    rows = array_ref.shape[0] // parts
    copies = [
        pltpu.make_async_copy(array_ref.at[pl.ds(k * rows, rows)], out_ref.at[pl.ds(k * rows, rows)], sem.at[k])
        for k in range(parts)
    ]
    for copy in copies:
        copy.start()
    for copy in copies:
        copy.wait()


def load(array, token):
    return pl.pallas_call(
        load_kernel,
        out_shape=jax.ShapeDtypeStruct(array.shape, array.dtype),
        in_specs=[IN_HBM, pl.BlockSpec(memory_space=pl.ANY)],
        out_specs=VMEM,
        scratch_shapes=[pltpu.SemaphoreType.DMA((8 if array.shape[0] % 128 == 0 else 1,))],
        compiler_params=pltpu.CompilerParams(vmem_limit_bytes=4 * 2**20),
        cost_estimate=SMALL,
    )(hbm(array), token)


def scores_of(target, feats):
    wide = feats.astype(jnp.float32)
    square = wide * wide
    lanes = min(128, square.shape[1])
    part = square[:, :lanes]
    for at in range(lanes, square.shape[1], lanes):
        part = part + square[:, at : at + lanes]
    half = 0.5 * jnp.sum(part.T, axis=0, keepdims=True)
    dots = lax.dot_general(target, feats, (((1,), (1,)), ((), ())), preferred_element_type=jnp.float32)
    return dots - half


def step_kernel(scale, count, first, last, exact, target_ref, *refs):
    pieces, refs = refs[:count], refs[count:]
    width = target_ref.shape[1]
    packed = jnp.concatenate([r[...] for r in pieces], axis=0)
    vecs = packed[:, width:]
    scores = scores_of(target_ref[...], packed[:, :width])
    top = jnp.max(scores, axis=1, keepdims=True)
    top = jnp.broadcast_to(top, (scores.shape[0], vecs.shape[1]))
    if not first:
        (before, denom, numer), refs = [r[...] for r in refs[:3]], refs[3:]
        top = jnp.maximum(before, top)
    across = scores.shape[1]
    level = jnp.concatenate([top] * pl.cdiv(across, top.shape[1]), axis=1)[:, :across]
    weights = jnp.exp2((scores - level) * scale)
    added = jnp.broadcast_to(jnp.sum(weights, axis=1, keepdims=True), top.shape)
    high = weights.astype(jnp.bfloat16)
    product = jnp.dot(high, vecs, preferred_element_type=jnp.float32)
    if exact:
        low = (weights - high.astype(jnp.float32)).astype(jnp.bfloat16)
        product = product + jnp.dot(low, vecs, preferred_element_type=jnp.float32)
    if not first:
        shrink = jnp.exp2((before - top) * scale)
        added = shrink * denom + added
        product = shrink * numer + product
    if not last:
        top_ref, denom_ref, numer_ref = refs
        top_ref[...] = top
        denom_ref[...] = added
        numer_ref[...] = product
        return
    current_ref, previous_ref, next_ref, column_ref = refs
    step = 2.0 / 0.05 * (product / added - 0.01 * current_ref[...]) - previous_ref[...]
    next_ref[...] = step
    column_ref[...] = jnp.sum(step * step, axis=0, keepdims=True)


def step(target, pieces, state, ends, scale, micros=0, exact=False):
    rows, width = target.shape
    cols = pieces[0].shape[1] - width
    whole = jax.ShapeDtypeStruct((rows, cols), jnp.float32)
    return pl.pallas_call(
        functools.partial(step_kernel, scale, len(pieces), not state, bool(ends), exact),
        out_shape=[whole, jax.ShapeDtypeStruct((1, cols), jnp.float32)] if ends else [whole] * 3,
        in_specs=[VMEM] * (1 + len(pieces) + len(state) + len(ends)),
        out_specs=[VMEM] * (2 if ends else 3),
        compiler_params=pltpu.CompilerParams(vmem_limit_bytes=20 * 2**20),
        cost_estimate=pl.CostEstimate(flops=1 + micros * 10**9, bytes_accessed=1, transcendentals=0),
    )(target, *pieces, *state, *ends)


def gather(shard, target, scale):
    n = lax.axis_size("tgt")
    if n & (n - 1) or n < 16:
        everything = lax.all_gather(shard, "tgt", axis=0, tiled=True)
        return target, [everything], []
    near, bit = shard, n // 2
    while bit > 8:
        near = jnp.concatenate([near, swap(near, bit)], axis=0)
        bit //= 2
    near_other = swap(near, 1)
    one = cross(near, 4, bit, True)
    later = tie(near, near_other)
    two = cross(later, 4, bit, False)
    around = [one, two] + [swap(later, k) for k in (2, 6)]
    target = load(target, later)
    place = lax.axis_index("tgt")
    far = jnp.where((place // 4 + place // bit) % 2 == 0, one, two)
    beyond = [swap_by_core(far, a, b) for a, b in ((2, 4), (4, 2), (6, 6))]
    state = step(target, [near, near_other] + around, [], [], scale, 20, True)
    early = swap(joined(around), 1)
    state = step(target, [early], state, [], scale, 20, True)
    others = [swap(joined(beyond[:2], state[0]), 1), swap(beyond[2], 1)]
    state = step(target, beyond, state, [], scale, 0)
    return target, others, state


def on_device(target_features, source_features, vectors, current, previous):
    rows, width = target_features.shape
    gamma = 0.25 / math.sqrt(width)
    scale = 2.0 * gamma * math.log2(math.e)
    target, pieces, state = gather(pack(source_features, vectors), target_features, scale)
    next_iter, column = step(target, pieces, state, [current, previous], scale)
    column_sq = total(column)
    total_rows = rows * lax.axis_size("tgt")
    return next_iter / jnp.sqrt(column_sq / total_rows + 1e-06)


def solution(mesh):
    return jax.shard_map(
        on_device,
        mesh=mesh,
        in_specs=(P(("groups", "tgt"), None),) * 5,
        out_specs=P(("groups", "tgt"), None),
        check_vma=False,
    )
```

```python
import functools
import math

import jax
import jax.numpy as jnp
from jax import lax
from jax.experimental import pallas as pl
from jax.experimental.pallas import tpu as pltpu
from jax.sharding import PartitionSpec as P

VMEM = pl.BlockSpec(memory_space=pltpu.VMEM)
SMALL = pl.CostEstimate(flops=1, bytes_accessed=1, transcendentals=0)
IN_HBM = pl.BlockSpec(memory_space=pltpu.HBM)


def hbm(x):
    return pltpu.with_memory_space_constraint(x, pltpu.HBM)


def swap(x, bits):
    n = lax.axis_size("tgt")
    return lax.ppermute(x, "tgt", [(i, i ^ bits) for i in range(n)])


def swap_by_core(x, first, second):
    n = lax.axis_size("tgt")
    return lax.ppermute(x, "tgt", [(i, i ^ (second if i % 2 else first)) for i in range(n)])


def cross(x, low, high, ends_first):
    n = lax.axis_size("tgt")
    pairs = []
    for i in range(n):
        at_end = (i // low + i // high) % 2 == 0
        pairs.append((i, i ^ (low if at_end == ends_first else high)))
    return lax.ppermute(x, "tgt", pairs)


def total(x):
    n = lax.axis_size("tgt")
    if n & (n - 1) or n < 16:
        return lax.psum(x, "tgt")
    x = x + swap(x, 1)
    one = swap_by_core(x, 4, 6)
    two = swap_by_core(x, 2, 4)
    x = jnp.where(lax.axis_index("tgt") % 2 == 0, x + one + two, one)
    x = x + swap(x, 1)
    bit = 8
    while bit < n:
        x = x + swap(x, bit)
        bit *= 2
    return x


def pack_kernel(feats_ref, vecs_ref, out_ref, sems):
    width = feats_ref.shape[1]
    first = pltpu.make_async_copy(feats_ref, out_ref.at[:, :width], sems.at[0])
    second = pltpu.make_async_copy(vecs_ref, out_ref.at[:, width:], sems.at[1])
    first.start()
    second.start()
    first.wait()
    second.wait()


def pack(feats, vecs):
    rows, width = feats.shape
    return pl.pallas_call(
        pack_kernel,
        out_shape=jax.ShapeDtypeStruct((rows, width + vecs.shape[1]), feats.dtype),
        in_specs=[IN_HBM] * 2,
        out_specs=VMEM,
        scratch_shapes=[pltpu.SemaphoreType.DMA((2,))],
        compiler_params=pltpu.CompilerParams(vmem_limit_bytes=4 * 2**20),
    )(hbm(feats), hbm(vecs))


def join_kernel(count, *refs):
    out_ref = refs[-1]
    at = 0
    for piece in refs[:count]:
        out_ref[at : at + piece.shape[0], :] = piece[...]
        at += piece.shape[0]


def joined(pieces, *tokens):
    rows = sum(p.shape[0] for p in pieces)
    return pl.pallas_call(
        functools.partial(join_kernel, len(pieces)),
        out_shape=jax.ShapeDtypeStruct((rows, pieces[0].shape[1]), pieces[0].dtype),
        in_specs=[VMEM] * len(pieces) + [pl.BlockSpec(memory_space=pl.ANY)] * len(tokens),
        out_specs=VMEM,
        compiler_params=pltpu.CompilerParams(vmem_limit_bytes=8 * 2**20),
        cost_estimate=SMALL,
    )(*pieces, *tokens)


def tie(x, *tokens):
    return joined([x], *tokens)


def load_kernel(array_ref, token_ref, out_ref, sem):
    del token_ref
    parts = sem.shape[0]
    rows = array_ref.shape[0] // parts
    copies = [
        pltpu.make_async_copy(array_ref.at[pl.ds(k * rows, rows)], out_ref.at[pl.ds(k * rows, rows)], sem.at[k])
        for k in range(parts)
    ]
    for copy in copies:
        copy.start()
    for copy in copies:
        copy.wait()


def load(array, token):
    return pl.pallas_call(
        load_kernel,
        out_shape=jax.ShapeDtypeStruct(array.shape, array.dtype),
        in_specs=[IN_HBM, pl.BlockSpec(memory_space=pl.ANY)],
        out_specs=VMEM,
        scratch_shapes=[pltpu.SemaphoreType.DMA((8 if array.shape[0] % 128 == 0 else 1,))],
        compiler_params=pltpu.CompilerParams(vmem_limit_bytes=4 * 2**20),
        cost_estimate=SMALL,
    )(hbm(array), token)


def scores_of(target, feats):
    wide = feats.astype(jnp.float32)
    square = wide * wide
    lanes = min(128, square.shape[1])
    part = square[:, :lanes]
    for at in range(lanes, square.shape[1], lanes):
        part = part + square[:, at : at + lanes]
    half = 0.5 * jnp.sum(part.T, axis=0, keepdims=True)
    dots = lax.dot_general(target, feats, (((1,), (1,)), ((), ())), preferred_element_type=jnp.float32)
    return dots - half


def step_kernel(scale, count, first, last, exact, target_ref, *refs):
    pieces, refs = refs[:count], refs[count:]
    width = target_ref.shape[1]
    packed = jnp.concatenate([r[...] for r in pieces], axis=0)
    vecs = packed[:, width:]
    scores = scores_of(target_ref[...], packed[:, :width])
    top = jnp.max(scores, axis=1, keepdims=True)
    top = jnp.broadcast_to(top, (scores.shape[0], vecs.shape[1]))
    if not first:
        (before, denom, numer), refs = [r[...] for r in refs[:3]], refs[3:]
        top = jnp.maximum(before, top)
    across = scores.shape[1]
    level = jnp.concatenate([top] * pl.cdiv(across, top.shape[1]), axis=1)[:, :across]
    weights = jnp.exp2((scores - level) * scale)
    added = jnp.broadcast_to(jnp.sum(weights, axis=1, keepdims=True), top.shape)
    high = weights.astype(jnp.bfloat16)
    product = jnp.dot(high, vecs, preferred_element_type=jnp.float32)
    if exact:
        low = (weights - high.astype(jnp.float32)).astype(jnp.bfloat16)
        product = product + jnp.dot(low, vecs, preferred_element_type=jnp.float32)
    if not first:
        shrink = jnp.exp2((before - top) * scale)
        added = shrink * denom + added
        product = shrink * numer + product
    if not last:
        top_ref, denom_ref, numer_ref = refs
        top_ref[...] = top
        denom_ref[...] = added
        numer_ref[...] = product
        return
    current_ref, previous_ref, next_ref, column_ref = refs
    step = 2.0 / 0.05 * (product / added - 0.01 * current_ref[...]) - previous_ref[...]
    next_ref[...] = step
    column_ref[...] = jnp.sum(step * step, axis=0, keepdims=True)


def step(target, pieces, state, ends, scale, micros=0, exact=False):
    rows, width = target.shape
    cols = pieces[0].shape[1] - width
    whole = jax.ShapeDtypeStruct((rows, cols), jnp.float32)
    return pl.pallas_call(
        functools.partial(step_kernel, scale, len(pieces), not state, bool(ends), exact),
        out_shape=[whole, jax.ShapeDtypeStruct((1, cols), jnp.float32)] if ends else [whole] * 3,
        in_specs=[VMEM] * (1 + len(pieces) + len(state) + len(ends)),
        out_specs=[VMEM] * (2 if ends else 3),
        compiler_params=pltpu.CompilerParams(vmem_limit_bytes=20 * 2**20),
        cost_estimate=pl.CostEstimate(flops=1 + micros * 10**9, bytes_accessed=1, transcendentals=0),
    )(target, *pieces, *state, *ends)


def gather(shard, target, scale):
    n = lax.axis_size("tgt")
    if n & (n - 1) or n < 16:
        everything = lax.all_gather(shard, "tgt", axis=0, tiled=True)
        return target, [everything], []
    near, bit = shard, n // 2
    while bit > 8:
        near = jnp.concatenate([near, swap(near, bit)], axis=0)
        bit //= 2
    near_other = swap(near, 1)
    one = cross(near, 4, bit, True)
    later = tie(near, near_other)
    two = cross(later, 4, bit, False)
    around = [one, two] + [swap(later, k) for k in (2, 6)]
    target = load(target, later)
    place = lax.axis_index("tgt")
    far = jnp.where((place // 4 + place // bit) % 2 == 0, one, two)
    beyond = [swap_by_core(far, a, b) for a, b in ((2, 4), (4, 2), (6, 6))]
    state = step(target, [near, near_other] + around, [], [], scale, 20, True)
    early = swap(joined(around), 1)
    state = step(target, [early], state, [], scale, 20, True)
    others = [swap(joined(beyond[:2], state[0]), 1), swap(beyond[2], 1)]
    state = step(target, beyond, state, [], scale, 0)
    return target, others, state


def on_device(target_features, source_features, vectors, current, previous):
    rows, width = target_features.shape
    gamma = 0.25 / math.sqrt(width)
    scale = 2.0 * gamma * math.log2(math.e)
    target, pieces, state = gather(pack(source_features, vectors), target_features, scale)
    next_iter, column = step(target, pieces, state, [current, previous], scale)
    column_sq = total(column)
    total_rows = rows * lax.axis_size("tgt")
    return next_iter / jnp.sqrt(column_sq / total_rows + 1e-06)


def solution(mesh):
    return jax.shard_map(
        on_device,
        mesh=mesh,
        in_specs=(P(("groups", "tgt"), None),) * 5,
        out_specs=P(("groups", "tgt"), None),
        check_vma=False,
    )
```

```python
import functools
import math

import jax
import jax.numpy as jnp
from jax import lax
from jax.experimental import pallas as pl
from jax.experimental.pallas import tpu as pltpu
from jax.sharding import PartitionSpec as P

VMEM = pl.BlockSpec(memory_space=pltpu.VMEM)
SMALL = pl.CostEstimate(flops=1, bytes_accessed=1, transcendentals=0)
IN_HBM = pl.BlockSpec(memory_space=pltpu.HBM)


def hbm(x):
    return pltpu.with_memory_space_constraint(x, pltpu.HBM)


def swap(x, bits):
    n = lax.axis_size("tgt")
    return lax.ppermute(x, "tgt", [(i, i ^ bits) for i in range(n)])


def swap_by_core(x, first, second):
    n = lax.axis_size("tgt")
    return lax.ppermute(x, "tgt", [(i, i ^ (second if i % 2 else first)) for i in range(n)])


def cross(x, low, high, ends_first):
    n = lax.axis_size("tgt")
    pairs = []
    for i in range(n):
        at_end = (i // low + i // high) % 2 == 0
        pairs.append((i, i ^ (low if at_end == ends_first else high)))
    return lax.ppermute(x, "tgt", pairs)


def total(x):
    n = lax.axis_size("tgt")
    if n & (n - 1) or n < 16:
        return lax.psum(x, "tgt")
    x = x + swap(x, 1)
    one = swap_by_core(x, 4, 6)
    two = swap_by_core(x, 2, 4)
    x = jnp.where(lax.axis_index("tgt") % 2 == 0, x + one + two, one)
    x = x + swap(x, 1)
    bit = 8
    while bit < n:
        x = x + swap(x, bit)
        bit *= 2
    return x


def pack_kernel(feats_ref, vecs_ref, out_ref, sems):
    width = feats_ref.shape[1]
    first = pltpu.make_async_copy(feats_ref, out_ref.at[:, :width], sems.at[0])
    second = pltpu.make_async_copy(vecs_ref, out_ref.at[:, width:], sems.at[1])
    first.start()
    second.start()
    first.wait()
    second.wait()


def pack(feats, vecs):
    rows, width = feats.shape
    return pl.pallas_call(
        pack_kernel,
        out_shape=jax.ShapeDtypeStruct((rows, width + vecs.shape[1]), feats.dtype),
        in_specs=[IN_HBM] * 2,
        out_specs=VMEM,
        scratch_shapes=[pltpu.SemaphoreType.DMA((2,))],
        compiler_params=pltpu.CompilerParams(vmem_limit_bytes=4 * 2**20),
    )(hbm(feats), hbm(vecs))


def join_kernel(count, *refs):
    out_ref = refs[-1]
    at = 0
    for piece in refs[:count]:
        out_ref[at : at + piece.shape[0], :] = piece[...]
        at += piece.shape[0]


def joined(pieces, *tokens):
    rows = sum(p.shape[0] for p in pieces)
    return pl.pallas_call(
        functools.partial(join_kernel, len(pieces)),
        out_shape=jax.ShapeDtypeStruct((rows, pieces[0].shape[1]), pieces[0].dtype),
        in_specs=[VMEM] * len(pieces) + [pl.BlockSpec(memory_space=pl.ANY)] * len(tokens),
        out_specs=VMEM,
        compiler_params=pltpu.CompilerParams(vmem_limit_bytes=8 * 2**20),
        cost_estimate=SMALL,
    )(*pieces, *tokens)


def tie(x, *tokens):
    return joined([x], *tokens)


def load_kernel(array_ref, token_ref, current_ref, previous_ref, out_ref, rest_ref, sem):
    del token_ref
    parts = sem.shape[0]
    rows = array_ref.shape[0] // parts
    copies = [
        pltpu.make_async_copy(array_ref.at[pl.ds(k * rows, rows)], out_ref.at[pl.ds(k * rows, rows)], sem.at[k])
        for k in range(parts)
    ]
    for copy in copies:
        copy.start()
    rest_ref[...] = 2.0 / 0.05 * 0.01 * current_ref[...] + previous_ref[...]
    for copy in copies:
        copy.wait()


def load(array, token, current, previous):
    return pl.pallas_call(
        load_kernel,
        out_shape=[jax.ShapeDtypeStruct(array.shape, array.dtype), jax.ShapeDtypeStruct(current.shape, current.dtype)],
        in_specs=[IN_HBM, pl.BlockSpec(memory_space=pl.ANY), VMEM, VMEM],
        out_specs=[VMEM] * 2,
        scratch_shapes=[pltpu.SemaphoreType.DMA((8 if array.shape[0] % 128 == 0 else 1,))],
        compiler_params=pltpu.CompilerParams(vmem_limit_bytes=8 * 2**20),
        cost_estimate=SMALL,
    )(hbm(array), token, current, previous)


def scores_of(target, feats):
    wide = feats.astype(jnp.float32)
    square = wide * wide
    lanes = min(128, square.shape[1])
    part = square[:, :lanes]
    for at in range(lanes, square.shape[1], lanes):
        part = part + square[:, at : at + lanes]
    half = 0.5 * jnp.sum(part.T, axis=0, keepdims=True)
    dots = lax.dot_general(target, feats, (((1,), (1,)), ((), ())), preferred_element_type=jnp.float32)
    return dots - half


def step_kernel(scale, count, first, last, exact, target_ref, *refs):
    pieces, refs = refs[:count], refs[count:]
    width = target_ref.shape[1]
    packed = jnp.concatenate([r[...] for r in pieces], axis=0)
    vecs = packed[:, width:]
    scores = scores_of(target_ref[...], packed[:, :width])
    top = jnp.max(scores, axis=1, keepdims=True)
    top = jnp.broadcast_to(top, (scores.shape[0], vecs.shape[1]))
    if not first:
        (before, denom, numer), refs = [r[...] for r in refs[:3]], refs[3:]
        top = jnp.maximum(before, top)
    across = scores.shape[1]
    level = jnp.concatenate([top] * pl.cdiv(across, top.shape[1]), axis=1)[:, :across]
    weights = jnp.exp2((scores - level) * scale)
    added = jnp.broadcast_to(jnp.sum(weights, axis=1, keepdims=True), top.shape)
    high = weights.astype(jnp.bfloat16)
    product = jnp.dot(high, vecs, preferred_element_type=jnp.float32)
    if exact:
        low = (weights - high.astype(jnp.float32)).astype(jnp.bfloat16)
        product = product + jnp.dot(low, vecs, preferred_element_type=jnp.float32)
    if not first:
        shrink = jnp.exp2((before - top) * scale)
        added = shrink * denom + added
        product = shrink * numer + product
    if not last:
        top_ref, denom_ref, numer_ref = refs
        top_ref[...] = top
        denom_ref[...] = added
        numer_ref[...] = product
        return
    rest_ref, next_ref, column_ref = refs
    step = 2.0 / 0.05 * (product / added) - rest_ref[...]
    next_ref[...] = step
    column_ref[...] = jnp.sum(step * step, axis=0, keepdims=True)


def step(target, pieces, state, ends, scale, micros=0, exact=False):
    rows, width = target.shape
    cols = pieces[0].shape[1] - width
    whole = jax.ShapeDtypeStruct((rows, cols), jnp.float32)
    return pl.pallas_call(
        functools.partial(step_kernel, scale, len(pieces), not state, bool(ends), exact),
        out_shape=[whole, jax.ShapeDtypeStruct((1, cols), jnp.float32)] if ends else [whole] * 3,
        in_specs=[VMEM] * (1 + len(pieces) + len(state) + len(ends)),
        out_specs=[VMEM] * (2 if ends else 3),
        compiler_params=pltpu.CompilerParams(vmem_limit_bytes=20 * 2**20),
        cost_estimate=pl.CostEstimate(flops=1 + micros * 10**9, bytes_accessed=1, transcendentals=0),
    )(target, *pieces, *state, *ends)


def gather(shard, target, current, previous, scale):
    n = lax.axis_size("tgt")
    if n & (n - 1) or n < 16:
        everything = lax.all_gather(shard, "tgt", axis=0, tiled=True)
        target, rest = load(target, shard, current, previous)
        return target, rest, [everything], []
    near, bit = shard, n // 2
    while bit > 8:
        near = jnp.concatenate([near, swap(near, bit)], axis=0)
        bit //= 2
    near_other = swap(near, 1)
    one = cross(near, 4, bit, True)
    later = tie(near, near_other)
    two = cross(later, 4, bit, False)
    around = [one, two] + [swap(later, k) for k in (2, 6)]
    target, rest = load(target, later, current, previous)
    place = lax.axis_index("tgt")
    far = jnp.where((place // 4 + place // bit) % 2 == 0, one, two)
    beyond = [swap_by_core(far, a, b) for a, b in ((2, 4), (4, 2), (6, 6))]
    state = step(target, [near, near_other] + around, [], [], scale, 20, True)
    early = swap(joined(around), 1)
    state = step(target, [early], state, [], scale, 20, True)
    others = [swap(joined(beyond[:2], state[0]), 1), swap(beyond[2], 1)]
    state = step(target, beyond, state, [], scale, 0)
    return target, rest, others, state


def on_device(target_features, source_features, vectors, current, previous):
    rows, width = target_features.shape
    gamma = 0.25 / math.sqrt(width)
    scale = 2.0 * gamma * math.log2(math.e)
    target, rest, pieces, state = gather(pack(source_features, vectors), target_features, current, previous, scale)
    next_iter, column = step(target, pieces, state, [rest], scale)
    column_sq = total(column)
    total_rows = rows * lax.axis_size("tgt")
    return next_iter / jnp.sqrt(column_sq / total_rows + 1e-06)


def solution(mesh):
    return jax.shard_map(
        on_device,
        mesh=mesh,
        in_specs=(P(("groups", "tgt"), None),) * 5,
        out_specs=P(("groups", "tgt"), None),
        check_vma=False,
    )
```

```python
import functools
import math

import jax
import jax.numpy as jnp
from jax import lax
from jax.experimental import pallas as pl
from jax.experimental.pallas import tpu as pltpu
from jax.sharding import PartitionSpec as P

VMEM = pl.BlockSpec(memory_space=pltpu.VMEM)
SMALL = pl.CostEstimate(flops=1, bytes_accessed=1, transcendentals=0)
IN_HBM = pl.BlockSpec(memory_space=pltpu.HBM)


def hbm(x):
    return pltpu.with_memory_space_constraint(x, pltpu.HBM)


def swap(x, bits):
    n = lax.axis_size("tgt")
    return lax.ppermute(x, "tgt", [(i, i ^ bits) for i in range(n)])


def swap_by_core(x, first, second):
    n = lax.axis_size("tgt")
    return lax.ppermute(x, "tgt", [(i, i ^ (second if i % 2 else first)) for i in range(n)])


def cross(x, low, high, ends_first):
    n = lax.axis_size("tgt")
    pairs = []
    for i in range(n):
        at_end = (i // low + i // high) % 2 == 0
        pairs.append((i, i ^ (low if at_end == ends_first else high)))
    return lax.ppermute(x, "tgt", pairs)


def total(x):
    n = lax.axis_size("tgt")
    if n & (n - 1) or n < 16:
        return lax.psum(x, "tgt")
    x = x + swap(x, 1)
    x = x + swap(x, 2)
    g0 = swap_by_core(x, 8, 12)
    g1 = swap_by_core(x, 4, 8)
    x = jnp.where(lax.axis_index("tgt") % 2 == 0, x + g0 + g1, g0)
    x = x + swap(x, 1)
    bit = 16
    while bit < n:
        x = x + swap(x, bit)
        bit *= 2
    return x


def pack_kernel(feats_ref, vecs_ref, out_ref, sems):
    width = feats_ref.shape[1]
    first = pltpu.make_async_copy(feats_ref, out_ref.at[:, :width], sems.at[0])
    second = pltpu.make_async_copy(vecs_ref, out_ref.at[:, width:], sems.at[1])
    first.start()
    second.start()
    first.wait()
    second.wait()


def pack(feats, vecs):
    rows, width = feats.shape
    return pl.pallas_call(
        pack_kernel,
        out_shape=jax.ShapeDtypeStruct((rows, width + vecs.shape[1]), feats.dtype),
        in_specs=[IN_HBM] * 2,
        out_specs=VMEM,
        scratch_shapes=[pltpu.SemaphoreType.DMA((2,))],
        compiler_params=pltpu.CompilerParams(vmem_limit_bytes=4 * 2**20),
    )(hbm(feats), hbm(vecs))


def join_kernel(count, *refs):
    out_ref = refs[-1]
    at = 0
    for piece in refs[:count]:
        out_ref[at : at + piece.shape[0], :] = piece[...]
        at += piece.shape[0]


def joined(pieces, *tokens):
    rows = sum(p.shape[0] for p in pieces)
    return pl.pallas_call(
        functools.partial(join_kernel, len(pieces)),
        out_shape=jax.ShapeDtypeStruct((rows, pieces[0].shape[1]), pieces[0].dtype),
        in_specs=[VMEM] * len(pieces) + [pl.BlockSpec(memory_space=pl.ANY)] * len(tokens),
        out_specs=VMEM,
        compiler_params=pltpu.CompilerParams(vmem_limit_bytes=8 * 2**20),
        cost_estimate=SMALL,
    )(*pieces, *tokens)


def tie(x, *tokens):
    return joined([x], *tokens)


def load_kernel(array_ref, token_ref, out_ref, sem):
    del token_ref
    parts = sem.shape[0]
    rows = array_ref.shape[0] // parts
    copies = [
        pltpu.make_async_copy(array_ref.at[pl.ds(k * rows, rows)], out_ref.at[pl.ds(k * rows, rows)], sem.at[k])
        for k in range(parts)
    ]
    for copy in copies:
        copy.start()
    for copy in copies:
        copy.wait()


def load(array, token):
    return pl.pallas_call(
        load_kernel,
        out_shape=jax.ShapeDtypeStruct(array.shape, array.dtype),
        in_specs=[IN_HBM, pl.BlockSpec(memory_space=pl.ANY)],
        out_specs=VMEM,
        scratch_shapes=[pltpu.SemaphoreType.DMA((8 if array.shape[0] % 128 == 0 else 1,))],
        compiler_params=pltpu.CompilerParams(vmem_limit_bytes=4 * 2**20),
        cost_estimate=SMALL,
    )(hbm(array), token)


def scores_of(target, feats):
    wide = feats.astype(jnp.float32)
    square = wide * wide
    lanes = min(128, square.shape[1])
    part = square[:, :lanes]
    for at in range(lanes, square.shape[1], lanes):
        part = part + square[:, at : at + lanes]
    half = 0.5 * jnp.sum(part.T, axis=0, keepdims=True)
    dots = lax.dot_general(target, feats, (((1,), (1,)), ((), ())), preferred_element_type=jnp.float32)
    return dots - half


def step_kernel(scale, count, first, last, exact, target_ref, *refs):
    pieces, refs = refs[:count], refs[count:]
    width = target_ref.shape[1]
    packed = jnp.concatenate([r[...] for r in pieces], axis=0)
    vecs = packed[:, width:]
    scores = scores_of(target_ref[...], packed[:, :width])
    top = jnp.max(scores, axis=1, keepdims=True)
    top = jnp.broadcast_to(top, (scores.shape[0], vecs.shape[1]))
    if not first:
        (before, denom, numer), refs = [r[...] for r in refs[:3]], refs[3:]
        top = jnp.maximum(before, top)
    across = scores.shape[1]
    level = jnp.concatenate([top] * pl.cdiv(across, top.shape[1]), axis=1)[:, :across]
    weights = jnp.exp2((scores - level) * scale)
    added = jnp.broadcast_to(jnp.sum(weights, axis=1, keepdims=True), top.shape)
    high = weights.astype(jnp.bfloat16)
    product = jnp.dot(high, vecs, preferred_element_type=jnp.float32)
    if exact:
        low = (weights - high.astype(jnp.float32)).astype(jnp.bfloat16)
        product = product + jnp.dot(low, vecs, preferred_element_type=jnp.float32)
    if not first:
        shrink = jnp.exp2((before - top) * scale)
        added = shrink * denom + added
        product = shrink * numer + product
    if not last:
        top_ref, denom_ref, numer_ref = refs
        top_ref[...] = top
        denom_ref[...] = added
        numer_ref[...] = product
        return
    current_ref, previous_ref, next_ref, column_ref = refs
    step = 2.0 / 0.05 * (product / added - 0.01 * current_ref[...]) - previous_ref[...]
    next_ref[...] = step
    column_ref[...] = jnp.sum(step * step, axis=0, keepdims=True)


def step(target, pieces, state, ends, scale, micros=0, exact=False):
    rows, width = target.shape
    cols = pieces[0].shape[1] - width
    whole = jax.ShapeDtypeStruct((rows, cols), jnp.float32)
    return pl.pallas_call(
        functools.partial(step_kernel, scale, len(pieces), not state, bool(ends), exact),
        out_shape=[whole, jax.ShapeDtypeStruct((1, cols), jnp.float32)] if ends else [whole] * 3,
        in_specs=[VMEM] * (1 + len(pieces) + len(state) + len(ends)),
        out_specs=[VMEM] * (2 if ends else 3),
        compiler_params=pltpu.CompilerParams(vmem_limit_bytes=20 * 2**20),
        cost_estimate=pl.CostEstimate(flops=1 + micros * 10**9, bytes_accessed=1, transcendentals=0),
    )(target, *pieces, *state, *ends)


def gather(shard, target, scale):
    n = lax.axis_size("tgt")
    if n & (n - 1) or n < 16:
        everything = lax.all_gather(shard, "tgt", axis=0, tiled=True)
        return target, [everything], []
    near, bit = shard, n // 2
    while bit > 8:
        near = jnp.concatenate([near, swap(near, bit)], axis=0)
        bit //= 2
    near_other = swap(near, 1)
    one = cross(near, 4, bit, True)
    later = tie(near, near_other)
    two = cross(later, 4, bit, False)
    around = [one, two] + [swap(later, k) for k in (2, 6)]
    target = load(target, later)
    place = lax.axis_index("tgt")
    far = jnp.where((place // 4 + place // bit) % 2 == 0, one, two)
    beyond = [swap_by_core(far, a, b) for a, b in ((2, 4), (4, 2), (6, 6))]
    state = step(target, [near, near_other] + around, [], [], scale, 20, True)
    early = swap(joined(around), 1)
    state = step(target, [early], state, [], scale, 20, True)
    others = [swap(joined(beyond[:2], state[0]), 1), swap(beyond[2], 1)]
    state = step(target, beyond, state, [], scale, 0)
    return target, others, state


def on_device(target_features, source_features, vectors, current, previous):
    rows, width = target_features.shape
    gamma = 0.25 / math.sqrt(width)
    scale = 2.0 * gamma * math.log2(math.e)
    target, pieces, state = gather(pack(source_features, vectors), target_features, scale)
    next_iter, column = step(target, pieces, state, [current, previous], scale)
    column_sq = total(column)
    total_rows = rows * lax.axis_size("tgt")
    return next_iter / jnp.sqrt(column_sq / total_rows + 1e-06)


def solution(mesh):
    return jax.shard_map(
        on_device,
        mesh=mesh,
        in_specs=(P(("groups", "tgt"), None),) * 5,
        out_specs=P(("groups", "tgt"), None),
        check_vma=False,
    )
```

```python
import functools
import math

import jax
import jax.numpy as jnp
from jax import lax
from jax.experimental import pallas as pl
from jax.experimental.pallas import tpu as pltpu
from jax.sharding import PartitionSpec as P

VMEM = pl.BlockSpec(memory_space=pltpu.VMEM)
SMALL = pl.CostEstimate(flops=1, bytes_accessed=1, transcendentals=0)
IN_HBM = pl.BlockSpec(memory_space=pltpu.HBM)


def hbm(x):
    return pltpu.with_memory_space_constraint(x, pltpu.HBM)


def swap(x, bits):
    n = lax.axis_size("tgt")
    return lax.ppermute(x, "tgt", [(i, i ^ bits) for i in range(n)])


def swap_by_core(x, first, second):
    n = lax.axis_size("tgt")
    return lax.ppermute(x, "tgt", [(i, i ^ (second if i % 2 else first)) for i in range(n)])


def cross(x, low, high, ends_first):
    n = lax.axis_size("tgt")
    pairs = []
    for i in range(n):
        at_end = (i // low + i // high) % 2 == 0
        pairs.append((i, i ^ (low if at_end == ends_first else high)))
    return lax.ppermute(x, "tgt", pairs)


def total(x):
    n = lax.axis_size("tgt")
    if n & (n - 1) or n < 16:
        return lax.psum(x, "tgt")
    x = x + swap(x, 1)
    one = swap_by_core(x, 4, 6)
    two = swap_by_core(x, 2, 4)
    x = jnp.where(lax.axis_index("tgt") % 2 == 0, x + one + two, one)
    x = x + swap(x, 1)
    bit = 8
    while bit < n:
        x = x + swap(x, bit)
        bit *= 2
    return x


def pack_kernel(feats_ref, vecs_ref, out_ref, sems):
    width = feats_ref.shape[1]
    first = pltpu.make_async_copy(feats_ref, out_ref.at[:, :width], sems.at[0])
    second = pltpu.make_async_copy(vecs_ref, out_ref.at[:, width:], sems.at[1])
    first.start()
    second.start()
    first.wait()
    second.wait()


def pack(feats, vecs):
    rows, width = feats.shape
    return pl.pallas_call(
        pack_kernel,
        out_shape=jax.ShapeDtypeStruct((rows, width + vecs.shape[1]), feats.dtype),
        in_specs=[IN_HBM] * 2,
        out_specs=VMEM,
        scratch_shapes=[pltpu.SemaphoreType.DMA((2,))],
        compiler_params=pltpu.CompilerParams(vmem_limit_bytes=4 * 2**20),
    )(hbm(feats), hbm(vecs))


def join_kernel(count, *refs):
    out_ref = refs[-1]
    at = 0
    for piece in refs[:count]:
        out_ref[at : at + piece.shape[0], :] = piece[...]
        at += piece.shape[0]


def joined(pieces, *tokens):
    rows = sum(p.shape[0] for p in pieces)
    return pl.pallas_call(
        functools.partial(join_kernel, len(pieces)),
        out_shape=jax.ShapeDtypeStruct((rows, pieces[0].shape[1]), pieces[0].dtype),
        in_specs=[VMEM] * len(pieces) + [pl.BlockSpec(memory_space=pl.ANY)] * len(tokens),
        out_specs=VMEM,
        compiler_params=pltpu.CompilerParams(vmem_limit_bytes=8 * 2**20),
        cost_estimate=SMALL,
    )(*pieces, *tokens)


def tie(x, *tokens):
    return joined([x], *tokens)


def load_kernel(array_ref, token_ref, out_ref, sem):
    del token_ref
    parts = sem.shape[0]
    rows = array_ref.shape[0] // parts
    copies = [
        pltpu.make_async_copy(array_ref.at[pl.ds(k * rows, rows)], out_ref.at[pl.ds(k * rows, rows)], sem.at[k])
        for k in range(parts)
    ]
    for copy in copies:
        copy.start()
    for copy in copies:
        copy.wait()


def load(array, token):
    return pl.pallas_call(
        load_kernel,
        out_shape=jax.ShapeDtypeStruct(array.shape, array.dtype),
        in_specs=[IN_HBM, pl.BlockSpec(memory_space=pl.ANY)],
        out_specs=VMEM,
        scratch_shapes=[pltpu.SemaphoreType.DMA((8 if array.shape[0] % 128 == 0 else 1,))],
        compiler_params=pltpu.CompilerParams(vmem_limit_bytes=4 * 2**20),
        cost_estimate=SMALL,
    )(hbm(array), token)


def scores_of(target, feats):
    wide = feats.astype(jnp.float32)
    square = wide * wide
    lanes = min(128, square.shape[1])
    part = square[:, :lanes]
    for at in range(lanes, square.shape[1], lanes):
        part = part + square[:, at : at + lanes]
    half = 0.5 * jnp.sum(part.T, axis=0, keepdims=True)
    dots = lax.dot_general(target, feats, (((1,), (1,)), ((), ())), preferred_element_type=jnp.float32)
    return dots - half


def step_kernel(scale, count, first, last, exact, target_ref, *refs):
    pieces, refs = refs[:count], refs[count:]
    width = target_ref.shape[1]
    packed = jnp.concatenate([r[...] for r in pieces], axis=0)
    vecs = packed[:, width:]
    scores = scores_of(target_ref[...], packed[:, :width])
    top = jnp.max(scores, axis=1, keepdims=True)
    top = jnp.broadcast_to(top, (scores.shape[0], vecs.shape[1]))
    if not first:
        (before, denom, numer), refs = [r[...] for r in refs[:3]], refs[3:]
        top = jnp.maximum(before, top)
    across = scores.shape[1]
    level = jnp.concatenate([top] * pl.cdiv(across, top.shape[1]), axis=1)[:, :across]
    weights = jnp.exp2((scores - level) * scale)
    added = jnp.broadcast_to(jnp.sum(weights, axis=1, keepdims=True), top.shape)
    high = weights.astype(jnp.bfloat16)
    product = jnp.dot(high, vecs, preferred_element_type=jnp.float32)
    if exact:
        low = (weights - high.astype(jnp.float32)).astype(jnp.bfloat16)
        product = product + jnp.dot(low, vecs, preferred_element_type=jnp.float32)
    if not first:
        shrink = jnp.exp2((before - top) * scale)
        added = shrink * denom + added
        product = shrink * numer + product
    if not last:
        top_ref, denom_ref, numer_ref = refs
        top_ref[...] = top
        denom_ref[...] = added
        numer_ref[...] = product
        return
    current_ref, previous_ref, next_ref, column_ref = refs
    step = 2.0 / 0.05 * (product / added - 0.01 * current_ref[...]) - previous_ref[...]
    next_ref[...] = step
    column_ref[...] = jnp.sum(step * step, axis=0, keepdims=True)


def step(target, pieces, state, ends, scale, micros=0, exact=False):
    rows, width = target.shape
    cols = pieces[0].shape[1] - width
    whole = jax.ShapeDtypeStruct((rows, cols), jnp.float32)
    return pl.pallas_call(
        functools.partial(step_kernel, scale, len(pieces), not state, bool(ends), exact),
        out_shape=[whole, jax.ShapeDtypeStruct((1, cols), jnp.float32)] if ends else [whole] * 3,
        in_specs=[VMEM] * (1 + len(pieces) + len(state) + len(ends)),
        out_specs=[VMEM] * (2 if ends else 3),
        compiler_params=pltpu.CompilerParams(vmem_limit_bytes=20 * 2**20),
        cost_estimate=pl.CostEstimate(flops=1 + micros * 10**9, bytes_accessed=1, transcendentals=0),
    )(target, *pieces, *state, *ends)


def gather(shard, target, scale):
    n = lax.axis_size("tgt")
    if n & (n - 1) or n < 16:
        everything = lax.all_gather(shard, "tgt", axis=0, tiled=True)
        return target, [everything], []
    near, bit = shard, n // 2
    while bit > 8:
        near = jnp.concatenate([near, swap(near, bit)], axis=0)
        bit //= 2
    near_other = swap(near, 1)
    one = cross(near, 4, bit, True)
    later = tie(near, near_other)
    two = cross(later, 4, bit, False)
    around = [one, two] + [swap(later, k) for k in (2, 6)]
    target = load(target, later)
    place = lax.axis_index("tgt")
    far = jnp.where((place // 4 + place // bit) % 2 == 0, one, two)
    beyond = [swap_by_core(far, a, b) for a, b in ((6, 4), (4, 2), (2, 6))]
    state = step(target, [near, near_other] + around, [], [], scale, 20, True)
    early = swap(joined(around), 1)
    state = step(target, [early], state, [], scale, 20, True)
    others = [swap(joined(beyond[:2], state[0]), 1), swap(beyond[2], 1)]
    state = step(target, beyond, state, [], scale, 0)
    return target, others, state


def on_device(target_features, source_features, vectors, current, previous):
    rows, width = target_features.shape
    gamma = 0.25 / math.sqrt(width)
    scale = 2.0 * gamma * math.log2(math.e)
    target, pieces, state = gather(pack(source_features, vectors), target_features, scale)
    next_iter, column = step(target, pieces, state, [current, previous], scale)
    column_sq = total(column)
    total_rows = rows * lax.axis_size("tgt")
    return next_iter / jnp.sqrt(column_sq / total_rows + 1e-06)


def solution(mesh):
    return jax.shard_map(
        on_device,
        mesh=mesh,
        in_specs=(P(("groups", "tgt"), None),) * 5,
        out_specs=P(("groups", "tgt"), None),
        check_vma=False,
    )
```
